32 devices in a mesh: grp: 2 (over x), dev: 16 (over z, y, core).
Axes of the slice: x: 2, y: 2, z: 4, core: 2. Of those that a mesh axis runs over, the one named last changes fastest.
Arguments:
- frames: bfloat16 [80, 64, 1408], P('dev'), may hold values from -100 to 100
- trained: int32 [80], replicated, may hold values from 0 to 3071, as said below
- frame_of: int32 [6144], P('dev'), may hold values from 0 to 3071, as said below
- token_cache: bfloat16 [6144, 1408], P('dev'), may hold values from -100 to 100
- norm_gains: float32 [2, 1408], P('grp'), may hold values from 0.1 to 1.9
- proj_weights: bfloat16 [2, 1408, 4224], P('grp'), may hold values from -4 to 4
- out_weights: bfloat16 [2, 1408, 1408], P('grp'), may hold values from -0.15625 to 0.15625
- patch_cotangent: bfloat16 [80, 64, 1408], P('dev'), may hold values from -0.119628906 to 0.119628906
- time_cotangent: bfloat16 [6144, 1408], P('dev'), may hold values from -6 to 6
Outputs:
- weight_grad: float32 [2, 1408, 1408], P('grp', 'dev')
The draws below stay inside these ranges and needn't reach their ends.
Inputs may be any that keep to these rules, and one draw needn't show every extreme that they name: `trained`: 80 different frames of the video; among them, for every k, the frames k * 192 and (k + 1) * 192 - 1. `frame_of`: never falls along the tokens; tokens 4 m to 4 m + 3 belong to frames 2 m and 2 m + 1, each frame having 1 to 3 tokens.
All inputs are finite; a program needn't handle non-finite values.
Results may differ from the reference program's by a relative error of at most 0.0078.
Values may be sent and summed in bfloat16 or wider, within the bound.
A program may use at most 192 MiB of HBM per device.

```python
import jax
import jax.numpy as jnp
from jax import lax

D = 1408
HEADS = 16
HEAD_DIM = 88
PATCHES = 64
SPAN = 128
TT_DEV = 384
FRAMES = 80
TOKENS = 6144
VIDEO_FRAMES = 3072


def paired_rows(key, rows, width):
    parts = jax.random.split(key, 1)
    return jax.random.normal(parts[0], (rows, width), jnp.float32)


def draw_frames(key, part):
    return paired_rows(jax.random.fold_in(key, 11), FRAMES * PATCHES, D).reshape(FRAMES, PATCHES, D).astype(jnp.bfloat16)


def draw_token_cache(key, part):
    return paired_rows(jax.random.fold_in(key, 12), TOKENS, D).astype(jnp.bfloat16)


def draw_trained(key, part):
    parts = jax.random.split(jax.random.fold_in(key, 13), 2)
    half_block = TT_DEV // 2
    video_pos = jnp.arange(VIDEO_FRAMES, dtype=jnp.int32)
    offset = video_pos % half_block
    forced = ((offset == 0) | (offset == half_block - 1)).astype(jnp.int32)
    ranks = jax.random.permutation(parts[0], VIDEO_FRAMES).astype(jnp.int32)
    scores = ranks + VIDEO_FRAMES * forced
    _, chosen = lax.top_k(scores, FRAMES)
    order = jax.random.permutation(parts[1], FRAMES)
    return chosen.astype(jnp.int32)[order]


def draw_frame_of(key, part):
    pairs = TOKENS // 4
    splits = jax.random.randint(jax.random.fold_in(key, 15), (pairs,), 1, 4).astype(jnp.int32)
    splits = splits.at[0].set(1)
    token_pos = jnp.arange(TOKENS, dtype=jnp.int32)
    pair_idx = token_pos // 4
    inside = token_pos % 4
    return (2 * pair_idx + (inside >= splits[pair_idx]).astype(jnp.int32)).astype(jnp.int32)


def draw_proj_weights(key, part):
    parts = jax.random.split(jax.random.fold_in(key, 14), 1)
    base = jax.random.normal(parts[0], (2, D, 3, HEADS, HEAD_DIM), jnp.float32) * D ** (-0.5)
    return jnp.clip(base.reshape(2, D, 3 * D), -4.0, 4.0).astype(jnp.bfloat16)


def levels(key, shape, pieces, least, top_value):
    loudness = 1.0
    for axis_at, blocks in pieces:
        draws = jax.random.uniform(jax.random.fold_in(jax.random.fold_in(key, 6), axis_at), (blocks,), jnp.float32, least / len(pieces), top_value / len(pieces))
        loudness = loudness * jnp.repeat(jnp.exp(draws), shape[axis_at] // blocks).reshape((-1,) + (1,) * (len(shape) - 1 - axis_at))
    return loudness


def centred(key, dims, deviation, most, cuts=(), kind=jnp.bfloat16):
    level = levels(key, dims, cuts, -0.22, 0.18) if cuts else 1.0
    drawn = jax.random.normal(key, dims, jnp.float32) * deviation * level
    return jnp.minimum(jnp.maximum(drawn, -most), most).astype(kind)


def setup_inputs(seed: int = 0) -> dict:
    streams_of = jax.random.split(jax.random.key(seed), 10)
    frames = draw_frames(jax.random.fold_in(streams_of[9], 71), 0)
    trained = draw_trained(jax.random.fold_in(streams_of[9], 71), 0)
    frame_of = draw_frame_of(jax.random.fold_in(streams_of[9], 71), 0)
    token_cache = draw_token_cache(jax.random.fold_in(streams_of[9], 71), 0)
    norm_gains = jnp.clip(1.0 + 0.18 * jax.random.normal(streams_of[4], (2, D), jnp.float32), 0.1, 1.9)
    proj_weights = draw_proj_weights(jax.random.fold_in(streams_of[9], 71), 0)
    out_weights = centred(streams_of[6], (2, D, D), D ** -0.5, 0.15625, ((0, 2),))
    patch_cotangent = centred(streams_of[7], (FRAMES, PATCHES, D), 0.02, 0.119628906, ((0, 16),))
    time_cotangent = centred(streams_of[8], (TOKENS, D), 1.0, 6.0, ((0, 16),))
    return {"frames": frames, "trained": trained, "frame_of": frame_of, "token_cache": token_cache, "norm_gains": norm_gains, "proj_weights": proj_weights, "out_weights": out_weights, "patch_cotangent": patch_cotangent, "time_cotangent": time_cotangent}


EPS = 1e-06
HIGH_PRECISION = lax.Precision.HIGHEST

def normalize(rows):
    inverse = lax.rsqrt(lax.optimization_barrier(jnp.mean(rows * rows, axis=-1, keepdims=True)) + EPS)
    return (rows * inverse, inverse)

def spatial_layer(frames, norm_gain, in_proj, out_proj):
    frame_count, patches, width = frames.shape
    rows = frames.reshape(frame_count * patches, width).astype(jnp.float32)
    scaled, _ = normalize(rows)
    normed = (scaled * norm_gain).astype(jnp.bfloat16)
    packed = jnp.dot(normed, in_proj, preferred_element_type=jnp.float32).astype(jnp.bfloat16)
    packed = packed.reshape(frame_count, patches, 3, HEADS, HEAD_DIM).astype(jnp.float32)
    attention_logits = jnp.einsum('fphd,fqhd->fhpq', packed[:, :, 0], packed[:, :, 1], precision=HIGH_PRECISION) * HEAD_DIM ** (-0.5)
    attention_probs = jax.nn.softmax(attention_logits, axis=-1).astype(jnp.bfloat16).astype(jnp.float32)
    attended_output = jnp.einsum('fhpq,fqhd->fphd', attention_probs, packed[:, :, 2], precision=HIGH_PRECISION)
    attended_output = attended_output.astype(jnp.bfloat16).reshape(frame_count * patches, width)
    output = rows + jnp.dot(attended_output, out_proj, preferred_element_type=jnp.float32)
    pooled = lax.optimization_barrier(jnp.mean(output.reshape(frame_count, patches, width), axis=1)).astype(jnp.bfloat16)
    return (pooled, attended_output)

def windows(array, nblocks):
    blocks = array.reshape(nblocks, SPAN, -1)
    zero = jnp.zeros_like(blocks[:1])
    padded = jnp.concatenate([zero, blocks, zero], axis=0)
    return jnp.concatenate([padded[:-2], padded[1:-1], padded[2:]], axis=1)

def unwindow(parts, nblocks):
    parts = parts.reshape(nblocks, 3, SPAN, -1)
    zero = jnp.zeros_like(parts[:1, 0])
    total = parts[:, 1] + jnp.concatenate([parts[1:, 0], zero], axis=0) + jnp.concatenate([zero, parts[:-1, 2]], axis=0)
    return total.reshape(nblocks * SPAN, -1)

def reference(frames, trained, frame_of, token_cache, norm_gains, proj_weights, out_weights, patch_cotangent, time_cotangent):
    pooled, spatial_mixed = spatial_layer(frames, norm_gains[0], proj_weights[0], out_weights[0])
    selector = (frame_of[:, None] == trained[None, :]).astype(jnp.bfloat16)
    inputs = token_cache.astype(jnp.float32) + jnp.dot(selector, pooled, preferred_element_type=jnp.float32)
    scaled, inverse = normalize(inputs)
    normed = (scaled * norm_gains[1]).astype(jnp.bfloat16)
    packed = jnp.dot(normed, proj_weights[1], preferred_element_type=jnp.float32).astype(jnp.bfloat16)
    token_total, width = inputs.shape
    nblocks = token_total // SPAN
    heads = packed.reshape(token_total, 3, HEADS, HEAD_DIM).transpose(1, 2, 0, 3)
    grad_mixed = jnp.dot(time_cotangent, out_weights[1].T, preferred_element_type=jnp.float32).astype(jnp.bfloat16)
    grad_heads = grad_mixed.reshape(token_total, HEADS, HEAD_DIM).transpose(1, 0, 2)
    win_pos = (jnp.arange(nblocks, dtype=jnp.int32)[:, None] - 1) * SPAN + jnp.arange(3 * SPAN, dtype=jnp.int32)[None, :]
    valid = (win_pos >= 0) & (win_pos < token_total)
    logit_scale = HEAD_DIM ** (-0.5)

    def head_pass(operands):
        query, key, value, grad = operands
        query_windows = query.reshape(nblocks, SPAN, HEAD_DIM).astype(jnp.float32)
        windowed_keys = windows(key, nblocks).astype(jnp.float32)
        windowed_values = windows(value, nblocks).astype(jnp.float32)
        attention_logits = jnp.einsum('uyi,uli->uyl', query_windows, windowed_keys, precision=HIGH_PRECISION) * logit_scale
        attention_logits = jnp.where(valid[:, None, :], attention_logits, -1e+30)
        row_top = lax.optimization_barrier(jnp.max(attention_logits, axis=-1, keepdims=True))
        log_total = row_top + jnp.log(lax.optimization_barrier(jnp.sum(jnp.exp(attention_logits - row_top), axis=-1, keepdims=True)))
        chances = jnp.exp(attention_logits - log_total)
        attention_probs = chances.astype(jnp.bfloat16).astype(jnp.float32)
        attended_output = jnp.einsum('jlf,jfe->jle', attention_probs, windowed_values, precision=HIGH_PRECISION).astype(jnp.bfloat16)
        block_gradient = grad.reshape(nblocks, SPAN, HEAD_DIM).astype(jnp.float32)
        row_delta = lax.optimization_barrier(jnp.sum(block_gradient * attended_output.astype(jnp.float32), axis=-1))
        probability_gradient = jnp.einsum('uyi,uli->uyl', block_gradient, windowed_values, precision=HIGH_PRECISION)
        logit_gradient = (chances * (probability_gradient - row_delta[..., None])).astype(jnp.bfloat16).astype(jnp.float32)
        query_gradient = jnp.einsum('jlf,jfe->jle', logit_gradient, windowed_keys, precision=HIGH_PRECISION) * logit_scale
        key_gradient = jnp.einsum('fpc,fpj->fcj', logit_gradient, query_windows, precision=HIGH_PRECISION) * logit_scale
        value_gradient = jnp.einsum('fpc,fpj->fcj', attention_probs, block_gradient, precision=HIGH_PRECISION)
        return (attended_output.reshape(token_total, HEAD_DIM), query_gradient.reshape(token_total, HEAD_DIM), unwindow(key_gradient, nblocks), unwindow(value_gradient, nblocks))
    mixed_heads, query_gradient, key_gradient, value_gradient = lax.map(head_pass, (heads[0], heads[1], heads[2], grad_heads))

    def merge_heads(block):
        return block.transpose(1, 0, 2).reshape(token_total, width)
    time_mixed = merge_heads(mixed_heads)
    grad_packed = jnp.concatenate([merge_heads(query_gradient), merge_heads(key_gradient), merge_heads(value_gradient)], axis=-1).astype(jnp.bfloat16)
    grad_normed = jnp.dot(grad_packed, proj_weights[1].T, preferred_element_type=jnp.float32)
    grad_scaled = grad_normed * norm_gains[1]
    grad_inputs = inverse * (grad_scaled - scaled * lax.optimization_barrier(jnp.mean(grad_scaled * scaled, axis=-1, keepdims=True))) + time_cotangent.astype(jnp.float32)
    frame_grads = jnp.dot(selector.astype(jnp.float32).T, grad_inputs, precision=HIGH_PRECISION)
    right_side = patch_cotangent.astype(jnp.float32) + frame_grads[:, None, :] / PATCHES
    spatial_grad = jnp.dot(spatial_mixed.astype(jnp.float32).T, right_side.reshape(-1, width), precision=HIGH_PRECISION)
    time_grad = jnp.dot(time_mixed.T, time_cotangent, preferred_element_type=jnp.float32)
    return jnp.stack([spatial_grad, time_grad])
```

```python
import functools

import jax
import jax.numpy as jnp
from jax import lax
from jax.experimental import pallas as pl
from jax.experimental.pallas import tpu as pltpu
from jax.sharding import PartitionSpec as P

HEADS = 16
HEAD_DIM = 88
SPAN = 128


EPS = 1e-06
HIGH_PRECISION = lax.Precision.HIGHEST


def from_behind(value, axis, steps):
    count = lax.axis_size(axis)
    initial, last = (max(0, -steps), min(count, count - steps))
    return lax.ppermute(value, axis, [(source, source + steps) for source in range(initial, last)])


def with_halo(array, sides, width):
    for axis, dim in sides:
        size, length = (lax.axis_size(axis), array.shape[dim])
        up = [(i, (i + 1) % size) for i in range(size - 1)]
        down = [(j, i) for i, j in up]
        last = lax.slice_in_dim(array, length - width, length, axis=dim)
        initial = lax.slice_in_dim(array, 0, width, axis=dim)
        before = lax.ppermute(last, axis, up)
        after = lax.ppermute(initial, axis, down)
        array = jnp.concatenate([before, array, after], axis=dim)
    return array


def normalize(rows):
    inverse = lax.rsqrt(jnp.mean(rows * rows, axis=-1, keepdims=True) + EPS)
    return (rows * inverse, inverse)


def when_true(flag, compute):

    def skipped():
        return jax.tree.map(jnp.zeros_like, compute())

    return lax.cond(flag, compute, skipped)


def contract_rows(left, right):
    return lax.dot_general(
        left, right, (((0,), (0,)), ((), ())), preferred_element_type=jnp.float32
    )


def contract_exact(left, right):
    return lax.dot_general(left, right, (((0,), (0,)), ((), ())), precision=HIGH_PRECISION)


def halves(value):
    high = lax.reduce_precision(value, 8, 7)
    return high.astype(jnp.bfloat16), (value - high).astype(jnp.bfloat16)


def lined(rows, lines):
    flat = rows.reshape(rows.shape[0], -1)
    return jnp.pad(flat, ((0, 0), (0, lines * 128 - flat.shape[1]))).reshape(-1, lines, 128)


def unlined(lines, count, width):
    flat = lines.reshape(lines.shape[0], -1)[:, : count * width]
    return flat.reshape(lines.shape[0] * count, width)


MESH = pl.DeviceIdType.MESH


def spread_kernel(count, own, out, send_sem, recv_sem):
    group = lax.axis_index("grp")
    me = lax.axis_index("dev")
    barrier = pltpu.get_barrier_semaphore()

    def copy(slot, target, group_to):
        return pltpu.make_async_remote_copy(
            src_ref=own,
            dst_ref=out.at[slot],
            send_sem=send_sem.at[target],
            recv_sem=recv_sem.at[slot],
            device_id=(group_to, target),
            device_id_type=MESH,
        )

    @pl.when(group == 1)
    def _():
        @pl.loop(0, count)
        def _(j):
            pl.semaphore_signal(barrier, inc=1, device_id=(0, j), device_id_type=MESH)

    @pl.when(group == 0)
    def _():
        pl.semaphore_wait(barrier, count)

        @pl.loop(0, count)
        def _(j):
            copy(me, lax.rem(me + j, count), 1).start()

        @pl.loop(0, count)
        def _(j):
            copy(me, lax.rem(me + j, count), 1).wait_send()

    @pl.when(group == 1)
    def _():
        @pl.loop(0, count)
        def _(j):
            copy(j, j, 0).wait_recv()


def spread(own, count):
    return pl.pallas_call(
        functools.partial(spread_kernel, count),
        out_shape=jax.ShapeDtypeStruct((count,) + own.shape, own.dtype),
        in_specs=[pl.BlockSpec(memory_space=pltpu.VMEM)],
        out_specs=pl.BlockSpec(memory_space=pltpu.VMEM),
        scratch_shapes=[pltpu.SemaphoreType.DMA((count,)), pltpu.SemaphoreType.DMA((count,))],
        compiler_params=pltpu.CompilerParams(
            collective_id=1, has_side_effects=True, vmem_limit_bytes=32 << 20
        ),
    )(own)


def collect_kernel(
    count, parts, sums, grads_out, sums_out, landed, part_send, part_recv, sum_send, sum_recv,
    grad_send, grad_recv,
):
    group = lax.axis_index("grp")
    me = lax.axis_index("dev")
    barrier = pltpu.get_barrier_semaphore()

    def part_copy(slot, target, group_to):
        return pltpu.make_async_remote_copy(
            src_ref=parts.at[target],
            dst_ref=landed.at[slot],
            send_sem=part_send.at[target],
            recv_sem=part_recv.at[slot],
            device_id=(group_to, target),
            device_id_type=MESH,
        )

    def sum_copy(slot, target):
        return pltpu.make_async_remote_copy(
            src_ref=sums,
            dst_ref=sums_out.at[slot],
            send_sem=sum_send.at[target],
            recv_sem=sum_recv.at[slot],
            device_id=(0, target),
            device_id_type=MESH,
        )

    def grad_copy(slot, target):
        return pltpu.make_async_remote_copy(
            src_ref=grads_out.at[me],
            dst_ref=grads_out.at[slot],
            send_sem=grad_send.at[target],
            recv_sem=grad_recv.at[slot],
            device_id=(0, target),
            device_id_type=MESH,
        )

    @pl.when(group == 0)
    def _():
        @pl.loop(0, count)
        def _(j):
            pl.semaphore_signal(barrier, inc=1, device_id=(1, j), device_id_type=MESH)

        @pl.loop(1, count)
        def _(j):
            pl.semaphore_signal(
                barrier, inc=1, device_id=(0, lax.rem(me + j, count)), device_id_type=MESH
            )

        pl.semaphore_wait(barrier, count - 1)

        @pl.loop(1, count)
        def _(j):
            sum_copy(me, lax.rem(me + j, count)).start()

        sums_out[me] = sums[...]

        @pl.loop(1, count)
        def _(j):
            other = lax.rem(me + j, count)
            sum_copy(other, other).wait_recv()

        @pl.loop(1, count)
        def _(j):
            sum_copy(me, lax.rem(me + j, count)).wait_send()

    @pl.when(group == 1)
    def _():
        pl.semaphore_wait(barrier, count)

        @pl.loop(0, count)
        def _(j):
            part_copy(me, lax.rem(me + j, count), 0).start()

        @pl.loop(0, count)
        def _(j):
            part_copy(me, lax.rem(me + j, count), 0).wait_send()

    @pl.when(group == 0)
    def _():
        @pl.loop(0, count)
        def _(j):
            part_copy(j, j, 1).wait_recv()

        total = jnp.sum(landed[...].astype(jnp.float32), axis=0)
        grads_out[me] = total.astype(jnp.bfloat16)

        @pl.loop(1, count)
        def _(j):
            grad_copy(me, lax.rem(me + j, count)).start()

        @pl.loop(1, count)
        def _(j):
            other = lax.rem(me + j, count)
            grad_copy(other, other).wait_recv()

        @pl.loop(1, count)
        def _(j):
            grad_copy(me, lax.rem(me + j, count)).wait_send()


def collect(parts, sums, count):
    vmem = pl.BlockSpec(memory_space=pltpu.VMEM)
    return pl.pallas_call(
        functools.partial(collect_kernel, count),
        out_shape=(
            jax.ShapeDtypeStruct(parts.shape, parts.dtype),
            jax.ShapeDtypeStruct((count,) + sums.shape, sums.dtype),
        ),
        in_specs=[vmem, vmem],
        out_specs=(vmem, vmem),
        scratch_shapes=[pltpu.VMEM(parts.shape, parts.dtype)]
        + [pltpu.SemaphoreType.DMA((count,)) for _ in range(6)],
        compiler_params=pltpu.CompilerParams(
            collective_id=2, has_side_effects=True, vmem_limit_bytes=32 << 20
        ),
    )(parts, sums)


def contract_cols(left, right):
    return lax.dot_general(
        left, right, (((1,), (1,)), ((), ())), preferred_element_type=jnp.float32
    )


def stack_windows(extended, count):
    return jnp.stack([extended[block * SPAN : (block + 3) * SPAN] for block in range(count)])


def shards(
    frames,
    trained,
    frame_of,
    token_cache,
    norm_gains,
    proj_weights,
    out_weights,
    patch_cotangent,
    time_cotangent,
):
    spatial = lax.axis_index("grp") == 0
    temporal = jnp.logical_not(spatial)
    norm_gain = norm_gains[0]
    in_proj = proj_weights[0]
    out_proj = out_weights[0]
    width = in_proj.shape[0]
    frame_count, patches, _ = frames.shape
    token_count = token_cache.shape[0]
    nblocks = token_count // SPAN
    score_scale = HEAD_DIM ** (-0.5)
    devices = lax.axis_size("dev")
    lines = -(-frame_count * width // 2048) * 16
    first_token = lax.axis_index("dev") * token_count
    token_total = lax.axis_size("dev") * token_count
    win_pos = (
        first_token
        + (jnp.arange(nblocks, dtype=jnp.int32)[:, None] - 1) * SPAN
        + jnp.arange(3 * SPAN, dtype=jnp.int32)[None, :]
    )
    win_valid = (win_pos >= 0) & (win_pos < token_total)

    def spatial_forward():
        rows = frames.reshape(frame_count * patches, width).astype(jnp.float32)
        scaled_rows, _ = normalize(rows)
        normed = (scaled_rows * norm_gain).astype(jnp.bfloat16)
        packed = jnp.dot(normed, in_proj, preferred_element_type=jnp.float32).astype(jnp.bfloat16)
        packed = packed.reshape(frame_count, patches, 3, HEADS, HEAD_DIM)
        attention_logits = (
            jnp.einsum(
                "fphd,fqhd->fhpq",
                packed[:, :, 0],
                packed[:, :, 1],
                preferred_element_type=jnp.float32,
            )
            * score_scale
        )
        attention_probs = jax.nn.softmax(attention_logits, axis=-1).astype(jnp.bfloat16)
        attended_output = jnp.einsum(
            "fhpq,fqhd->fphd", attention_probs, packed[:, :, 2], preferred_element_type=jnp.float32
        )
        attended_output = attended_output.astype(jnp.bfloat16).reshape(frame_count * patches, width)
        sums = jnp.sum(
            attended_output.reshape(frame_count, patches, width).astype(jnp.float32), axis=1
        )
        both = jnp.dot(
            jnp.concatenate(halves(sums), axis=0), out_proj, preferred_element_type=jnp.float32
        )
        carried = jnp.mean(rows.reshape(frame_count, patches, width), axis=1)
        pooled = carried + (both[:frame_count] + both[frame_count:]) / patches
        pooled = lined(pooled.astype(jnp.bfloat16).reshape(1, frame_count * width), lines)[0]
        grad_mixed = jnp.zeros((token_count, width), jnp.bfloat16)
        return (pooled, attended_output, sums, grad_mixed)

    def ahead():
        grad_mixed = contract_cols(time_cotangent, out_proj).astype(jnp.bfloat16)
        return (
            jnp.zeros((lines, 128), jnp.bfloat16),
            jnp.zeros((frame_count * patches, width), jnp.bfloat16),
            jnp.zeros((frame_count, width), jnp.float32),
            grad_mixed,
        )

    pooled, spatial_mixed, sums, grad_mixed = lax.cond(spatial, spatial_forward, ahead)
    arrived = unlined(spread(pooled, devices), frame_count, width)

    def temporal_front():
        selector = (frame_of[:, None] == trained[None, :]).astype(jnp.bfloat16)
        inputs = token_cache.astype(jnp.float32) + jnp.dot(
            selector, arrived, preferred_element_type=jnp.float32
        )
        scaled_rows, inverse = normalize(inputs)
        normed = (scaled_rows * norm_gain).astype(jnp.bfloat16)
        packed = jnp.dot(normed, in_proj, preferred_element_type=jnp.float32).astype(jnp.bfloat16)
        return (selector, scaled_rows, inverse, packed[:, :width], packed[:, width:])

    selector, scaled_rows, inverse, queries, key_value = when_true(temporal, temporal_front)
    extended = with_halo(key_value, (("dev", 0),), SPAN)
    key_window = stack_windows(extended, nblocks)
    key_heads = key_window[..., :width].reshape(nblocks, 3 * SPAN, HEADS, HEAD_DIM)
    value_heads = key_window[..., width:].reshape(nblocks, 3 * SPAN, HEADS, HEAD_DIM)
    query_heads = queries.reshape(nblocks, SPAN, HEADS, HEAD_DIM)

    def temporal_attend():
        attention_logits = (
            jnp.einsum(
                "bqhd,bkhd->bhqk", query_heads, key_heads, preferred_element_type=jnp.float32
            )
            * score_scale
        )
        attention_logits = jnp.where(win_valid[:, None, None, :], attention_logits, -1e30)
        row_top = jnp.max(attention_logits, axis=-1, keepdims=True)
        log_total = row_top + jnp.log(
            jnp.sum(jnp.exp(attention_logits - row_top), axis=-1, keepdims=True)
        )
        chances = jnp.exp(attention_logits - log_total)
        chance_weights = chances.astype(jnp.bfloat16)
        attended_output = jnp.einsum(
            "bhqk,bkhd->bqhd", chance_weights, value_heads, preferred_element_type=jnp.float32
        )
        return (
            chances,
            chance_weights,
            log_total[..., 0],
            attended_output.astype(jnp.bfloat16).reshape(token_count, width),
        )

    chances, chance_weights, log_total, time_mixed = when_true(temporal, temporal_attend)

    def from_frames():
        return contract_rows(
            spatial_mixed, patch_cotangent.reshape(frame_count * patches, width)
        ).astype(jnp.bfloat16)

    def from_tokens():
        return contract_rows(time_mixed, time_cotangent).astype(jnp.bfloat16)

    weight_part = lax.psum_scatter(
        lax.cond(spatial, from_frames, from_tokens), "dev", scatter_dimension=0, tiled=True
    ).astype(jnp.float32)

    def temporal_grads():
        grad_heads = grad_mixed.reshape(nblocks, SPAN, HEADS, HEAD_DIM)
        mixed_heads = time_mixed.reshape(nblocks, SPAN, HEADS, HEAD_DIM)
        row_delta = jnp.sum(
            grad_heads.astype(jnp.float32) * mixed_heads.astype(jnp.float32), axis=-1
        ).transpose(0, 2, 1)
        probability_gradient = jnp.einsum(
            "bqhd,bkhd->bhqk", grad_heads, value_heads, preferred_element_type=jnp.float32
        )
        logit_gradient = (chances * (probability_gradient - row_delta[..., None])).astype(
            jnp.bfloat16
        )
        query_gradient = (
            jnp.einsum(
                "bhqk,bkhd->bqhd", logit_gradient, key_heads, preferred_element_type=jnp.float32
            )
            * score_scale
        )
        return (row_delta, logit_gradient, query_gradient.reshape(token_count, width))

    row_delta, logit_gradient, query_gradient = when_true(temporal, temporal_grads)
    stats = jnp.concatenate(
        [
            log_total.transpose(0, 2, 1).reshape(token_count, HEADS),
            row_delta.transpose(0, 2, 1).reshape(token_count, HEADS),
        ],
        axis=-1,
    )
    near_stats = with_halo(stats, (("dev", 0),), SPAN)
    near_rows = with_halo(jnp.concatenate([queries, grad_mixed], axis=-1), (("dev", 0),), SPAN)

    def rim_keys():
        row_window = stack_windows(near_rows, nblocks)
        stat_window = stack_windows(near_stats, nblocks)
        query_part = row_window[..., :width].reshape(nblocks, 3 * SPAN, HEADS, HEAD_DIM)
        grad_part = row_window[..., width:].reshape(nblocks, 3 * SPAN, HEADS, HEAD_DIM)
        totals = stat_window[..., :HEADS].transpose(0, 2, 1)
        deltas = stat_window[..., HEADS:].transpose(0, 2, 1)
        own_keys = key_value[:, :width].reshape(nblocks, SPAN, HEADS, HEAD_DIM)
        own_values = key_value[:, width:].reshape(nblocks, SPAN, HEADS, HEAD_DIM)
        attention_logits = (
            jnp.einsum("bqhd,bkhd->bhqk", query_part, own_keys, preferred_element_type=jnp.float32)
            * score_scale
        )
        again = jnp.where(
            win_valid[:, None, :, None],
            jnp.exp(
                jnp.where(win_valid[:, None, :, None], attention_logits - totals[..., None], 0.0)
            ),
            0.0,
        )
        probability_gradient = jnp.einsum(
            "bqhd,bkhd->bhqk", grad_part, own_values, preferred_element_type=jnp.float32
        )
        part_score = (again * (probability_gradient - deltas[..., None])).astype(jnp.bfloat16)
        key_gradient = (
            jnp.einsum(
                "bhqk,bqhd->bkhd", part_score, query_part, preferred_element_type=jnp.float32
            )
            * score_scale
        )
        value_gradient = jnp.einsum(
            "bhqk,bqhd->bkhd",
            again.astype(jnp.bfloat16),
            grad_part,
            preferred_element_type=jnp.float32,
        )
        return jnp.concatenate(
            [key_gradient.reshape(token_count, width), value_gradient.reshape(token_count, width)],
            axis=-1,
        )

    key_grads = when_true(temporal, rim_keys)

    def temporal_back():
        grad_packed = jnp.concatenate([query_gradient, key_grads], axis=-1).astype(jnp.bfloat16)
        grad_scaled = contract_cols(grad_packed, in_proj) * norm_gain
        grad_inputs = inverse * (
            grad_scaled - scaled_rows * jnp.mean(grad_scaled * scaled_rows, axis=-1, keepdims=True)
        ) + time_cotangent.astype(jnp.float32)
        high, low = halves(grad_inputs)
        grads = contract_rows(selector, high) + contract_rows(selector, low)
        return lined(grads.astype(jnp.bfloat16).reshape(devices, frame_count * width), lines)

    parts = when_true(temporal, temporal_back)
    grad_lines, sum_lines = collect(
        parts, lined(sums.reshape(1, frame_count * width), lines)[0], devices
    )

    def from_pooled():
        frame_grads = unlined(grad_lines, frame_count, width).astype(jnp.float32)
        all_sums = unlined(sum_lines, frame_count, width)
        share = width // devices
        own_sums = lax.dynamic_slice_in_dim(
            all_sums, lax.axis_index("dev") * share, share, axis=1
        )
        return weight_part + contract_exact(own_sums, frame_grads) / patches

    return lax.cond(spatial, from_pooled, lambda: weight_part)[None]


def solution(mesh):
    in_specs = (
        P("dev", None, None),
        P(),
        P("dev"),
        P("dev", None),
        P("grp", None),
        P("grp", None, None),
        P("grp", None, None),
        P("dev", None, None),
        P("dev", None),
    )
    out_specs = P("grp", "dev", None)
    return jax.shard_map(shards, mesh=mesh, in_specs=in_specs, out_specs=out_specs, check_vma=False)
```

```python
import functools

import jax
import jax.numpy as jnp
from jax import lax
from jax.experimental import pallas as pl
from jax.experimental.pallas import tpu as pltpu
from jax.sharding import PartitionSpec as P

HEADS = 16
HEAD_DIM = 88
SPAN = 128


EPS = 1e-06
HIGH_PRECISION = lax.Precision.HIGHEST


def neighbours(array, rows):
    count = lax.axis_size("dev")
    length = array.shape[0]
    up = [(count + i, count + i + 1) for i in range(count - 1)]
    down = [(target, source) for source, target in up]
    before = lax.ppermute(array[length - rows :], ("grp", "dev"), up)
    after = lax.ppermute(array[:rows], ("grp", "dev"), down)
    return jnp.concatenate([before, array, after], axis=0)


def normalize(rows):
    inverse = lax.rsqrt(jnp.mean(rows * rows, axis=-1, keepdims=True) + EPS)
    return (rows * inverse, inverse)


def when_true(flag, compute):

    def skipped():
        return jax.tree.map(jnp.zeros_like, compute())

    return lax.cond(flag, compute, skipped)


def contract_rows(left, right):
    return lax.dot_general(
        left, right, (((0,), (0,)), ((), ())), preferred_element_type=jnp.float32
    )


def contract_exact(left, right):
    return lax.dot_general(left, right, (((0,), (0,)), ((), ())), precision=HIGH_PRECISION)


def halves(value):
    high = lax.reduce_precision(value, 8, 7)
    return high.astype(jnp.bfloat16), (value - high).astype(jnp.bfloat16)


def lined(rows, lines):
    flat = rows.reshape(rows.shape[0], -1)
    return jnp.pad(flat, ((0, 0), (0, lines * 128 - flat.shape[1]))).reshape(-1, lines, 128)


def unlined(lines, count, width):
    flat = lines.reshape(lines.shape[0], -1)[:, : count * width]
    return flat.reshape(lines.shape[0] * count, width)


MESH = pl.DeviceIdType.MESH


def spread_kernel(count, own, out, send_sem, recv_sem):
    group = lax.axis_index("grp")
    me = lax.axis_index("dev")
    barrier = pltpu.get_barrier_semaphore()

    def copy(slot, target, group_to):
        return pltpu.make_async_remote_copy(
            src_ref=own,
            dst_ref=out.at[slot],
            send_sem=send_sem.at[target],
            recv_sem=recv_sem.at[slot],
            device_id=(group_to, target),
            device_id_type=MESH,
        )

    @pl.when(group == 1)
    def _():
        @pl.loop(0, count)
        def _(j):
            pl.semaphore_signal(barrier, inc=1, device_id=(0, j), device_id_type=MESH)

    @pl.when(group == 0)
    def _():
        pl.semaphore_wait(barrier, count)

        @pl.loop(0, count)
        def _(j):
            copy(me, lax.rem(me + j, count), 1).start()

        @pl.loop(0, count)
        def _(j):
            copy(me, lax.rem(me + j, count), 1).wait_send()

    @pl.when(group == 1)
    def _():
        @pl.loop(0, count)
        def _(j):
            copy(j, j, 0).wait_recv()


def spread(own, count):
    return pl.pallas_call(
        functools.partial(spread_kernel, count),
        out_shape=jax.ShapeDtypeStruct((count,) + own.shape, own.dtype),
        in_specs=[pl.BlockSpec(memory_space=pltpu.VMEM)],
        out_specs=pl.BlockSpec(memory_space=pltpu.VMEM),
        scratch_shapes=[pltpu.SemaphoreType.DMA((count,)), pltpu.SemaphoreType.DMA((count,))],
        compiler_params=pltpu.CompilerParams(
            collective_id=1, has_side_effects=True, vmem_limit_bytes=32 << 20
        ),
    )(own)


def collect_kernel(
    count, parts, sums, grads_out, sums_out, landed, part_send, part_recv, sum_send, sum_recv,
    grad_send, grad_recv,
):
    group = lax.axis_index("grp")
    me = lax.axis_index("dev")
    barrier = pltpu.get_barrier_semaphore()

    def part_copy(slot, target, group_to):
        return pltpu.make_async_remote_copy(
            src_ref=parts.at[target],
            dst_ref=landed.at[slot],
            send_sem=part_send.at[target],
            recv_sem=part_recv.at[slot],
            device_id=(group_to, target),
            device_id_type=MESH,
        )

    def sum_copy(slot, target):
        return pltpu.make_async_remote_copy(
            src_ref=sums,
            dst_ref=sums_out.at[slot],
            send_sem=sum_send.at[target],
            recv_sem=sum_recv.at[slot],
            device_id=(0, target),
            device_id_type=MESH,
        )

    def grad_copy(slot, target):
        return pltpu.make_async_remote_copy(
            src_ref=grads_out.at[me],
            dst_ref=grads_out.at[slot],
            send_sem=grad_send.at[target],
            recv_sem=grad_recv.at[slot],
            device_id=(0, target),
            device_id_type=MESH,
        )

    @pl.when(group == 0)
    def _():
        @pl.loop(0, count)
        def _(j):
            pl.semaphore_signal(barrier, inc=1, device_id=(1, j), device_id_type=MESH)

        @pl.loop(1, count)
        def _(j):
            pl.semaphore_signal(
                barrier, inc=1, device_id=(0, lax.rem(me + j, count)), device_id_type=MESH
            )

        pl.semaphore_wait(barrier, count - 1)

        @pl.loop(1, count)
        def _(j):
            sum_copy(me, lax.rem(me + j, count)).start()

        sums_out[me] = sums[...]

        @pl.loop(1, count)
        def _(j):
            other = lax.rem(me + j, count)
            sum_copy(other, other).wait_recv()

        @pl.loop(1, count)
        def _(j):
            sum_copy(me, lax.rem(me + j, count)).wait_send()

    @pl.when(group == 1)
    def _():
        pl.semaphore_wait(barrier, count)

        @pl.loop(0, count)
        def _(j):
            part_copy(me, lax.rem(me + j, count), 0).start()

        @pl.loop(0, count)
        def _(j):
            part_copy(me, lax.rem(me + j, count), 0).wait_send()

    @pl.when(group == 0)
    def _():
        @pl.loop(0, count)
        def _(j):
            part_copy(j, j, 1).wait_recv()

        total = jnp.sum(landed[...].astype(jnp.float32), axis=0)
        grads_out[me] = total.astype(jnp.bfloat16)

        @pl.loop(1, count)
        def _(j):
            grad_copy(me, lax.rem(me + j, count)).start()

        @pl.loop(1, count)
        def _(j):
            other = lax.rem(me + j, count)
            grad_copy(other, other).wait_recv()

        @pl.loop(1, count)
        def _(j):
            grad_copy(me, lax.rem(me + j, count)).wait_send()


def collect(parts, sums, count):
    vmem = pl.BlockSpec(memory_space=pltpu.VMEM)
    return pl.pallas_call(
        functools.partial(collect_kernel, count),
        out_shape=(
            jax.ShapeDtypeStruct(parts.shape, parts.dtype),
            jax.ShapeDtypeStruct((count,) + sums.shape, sums.dtype),
        ),
        in_specs=[vmem, vmem],
        out_specs=(vmem, vmem),
        scratch_shapes=[pltpu.VMEM(parts.shape, parts.dtype)]
        + [pltpu.SemaphoreType.DMA((count,)) for _ in range(6)],
        compiler_params=pltpu.CompilerParams(
            collective_id=2, has_side_effects=True, vmem_limit_bytes=32 << 20
        ),
    )(parts, sums)


def contract_cols(left, right):
    return lax.dot_general(
        left, right, (((1,), (1,)), ((), ())), preferred_element_type=jnp.float32
    )


def dot_cols(left, right):
    return lax.dot_general(
        left, right, (((1,), (1,)), ((), ())), preferred_element_type=jnp.float32
    )


def dot_rows(left, right):
    return lax.dot_general(
        left, right, (((0,), (0,)), ((), ())), preferred_element_type=jnp.float32
    )


def dot_plain(left, right):
    return jnp.dot(left, right, preferred_element_type=jnp.float32)


SCALE = HEAD_DIM ** (-0.5)
WINDOW = 256


def block(index, count=1):
    return slice(index * SPAN, (index + count) * SPAN)


def head_window(head, width):
    first = head * HEAD_DIM
    start = pl.multiple_of(jnp.minimum(first // 128, (width - WINDOW) // 128) * 128, 128)
    lane = lax.broadcasted_iota(jnp.int32, (1, WINDOW), 1) + start
    return start, (lane >= first) & (lane < first + HEAD_DIM)


def blend(ref, rows, columns, mask, value):
    old = ref[rows, columns].astype(jnp.float32)
    ref[rows, columns] = jnp.where(mask, value, old).astype(ref.dtype)


def attend_kernel(packed, grad, bias, mixed, log_total, row_delta):
    width = grad.shape[1]
    blocks = grad.shape[0] // SPAN
    lanes = lax.broadcasted_iota(jnp.int32, (1, 128), 1)

    def one_head(head, carry):
        start, mask = head_window(head, width)
        keep = mask.astype(jnp.float32).astype(jnp.bfloat16)
        here = pl.ds(start, WINDOW)
        key_at = pl.ds(pl.multiple_of(start + width, 128), WINDOW)
        value_at = pl.ds(pl.multiple_of(start + 2 * width, 128), WINDOW)
        for i in range(blocks):
            query = packed[block(i + 1), here] * keep
            logits = dot_cols(query, packed[block(i, 3), key_at]) * SCALE + bias[:, block(i, 3)]
            top = jnp.max(logits, axis=-1, keepdims=True)
            raised = jnp.exp(logits - top)
            total = jnp.sum(raised, axis=-1, keepdims=True)
            chances = (raised / total).astype(jnp.bfloat16)
            value = dot_plain(chances, packed[block(i, 3), value_at])
            rounded = value.astype(jnp.bfloat16).astype(jnp.float32)
            product = grad[block(i), here].astype(jnp.float32) * rounded
            delta = jnp.sum(jnp.where(mask, product, 0.0), axis=-1, keepdims=True)
            own = lanes == head
            every = slice(0, 128)
            blend(log_total, block(i), every, own, top + jnp.log(total))
            blend(row_delta, block(i), every, own, delta)
            if 1 <= i < blocks - 1:
                blend(mixed, block(i - 1), here, mask, value)
        return carry

    lax.fori_loop(0, HEADS, one_head, 0, unroll=2)


def grads_kernel(packed, grad, bias, log_total, row_delta, out):
    width = grad.shape[1]
    blocks = grad.shape[0] // SPAN
    lanes = lax.broadcasted_iota(jnp.int32, (1, 128), 1)

    def one_head(head, carry):
        start, mask = head_window(head, width)
        keep = mask.astype(jnp.float32).astype(jnp.bfloat16)
        here = pl.ds(start, WINDOW)
        key_at = pl.ds(pl.multiple_of(start + width, 128), WINDOW)
        value_at = pl.ds(pl.multiple_of(start + 2 * width, 128), WINDOW)
        own = lanes == head
        query = packed[block(1, blocks), here] * keep
        cotangent = grad[:, here] * keep
        chance_of, grad_of = {}, {}
        for i in range(blocks):
            first, span = max(i - 1, 1), 3
            if i == 0:
                first, span = 1, 1
            elif i == blocks - 1:
                first, span = blocks - 2, 1
            else:
                first = i - 1
            at = block(first + 1, span)
            inside = bias[:, at] if span == 3 else bias[:, block(i + 1)]
            total = jnp.sum(jnp.where(own, log_total[block(i), :], 0.0), axis=-1, keepdims=True)
            delta = jnp.sum(jnp.where(own, row_delta[block(i), :], 0.0), axis=-1, keepdims=True)
            keys = packed[at, key_at]
            logits = dot_cols(query[block(i)], keys) * SCALE + inside
            chances = jnp.exp(logits - total)
            slope = dot_cols(cotangent[block(i)], packed[at, value_at])
            logit_grad = (chances * (slope - delta)).astype(jnp.bfloat16)
            chances = chances.astype(jnp.bfloat16)
            for step in range(span):
                chance_of[i, first + step] = chances[:, block(step)]
                grad_of[i, first + step] = logit_grad[:, block(step)]
            if span == 3:
                blend(out, block(i - 1), here, mask, dot_plain(logit_grad, keys) * SCALE)
        for j in range(1, blocks - 1):
            rows = block(j - 1, 3)
            near = range(j - 1, j + 2)
            scores = jnp.concatenate([grad_of[i, j] for i in near], axis=0)
            blend(out, block(j - 1), key_at, mask, dot_rows(scores, query[rows]) * SCALE)
            weights = jnp.concatenate([chance_of[i, j] for i in near], axis=0)
            blend(out, block(j - 1), value_at, mask, dot_rows(weights, cotangent[rows]))
        return carry

    lax.fori_loop(0, HEADS, one_head, 0, unroll=2)


def local_call(kernel, out_shape, *operands):
    return pl.pallas_call(
        kernel,
        out_shape=out_shape,
        in_specs=[pl.BlockSpec(memory_space=pltpu.VMEM)] * len(operands),
        out_specs=jax.tree.map(lambda _: pl.BlockSpec(memory_space=pltpu.VMEM), out_shape),
        compiler_params=pltpu.CompilerParams(vmem_limit_bytes=48 << 20),
    )(*operands)


def shards(
    frames,
    trained,
    frame_of,
    token_cache,
    norm_gains,
    proj_weights,
    out_weights,
    patch_cotangent,
    time_cotangent,
):
    spatial = lax.axis_index("grp") == 0
    temporal = jnp.logical_not(spatial)
    norm_gain = norm_gains[0]
    in_proj = proj_weights[0]
    out_proj = out_weights[0]
    width = in_proj.shape[0]
    frame_count, patches, _ = frames.shape
    token_count = token_cache.shape[0]
    devices = lax.axis_size("dev")
    lines = -(-frame_count * width // 2048) * 16
    blocks = token_count // SPAN
    near_tokens = neighbours(token_cache, 2 * SPAN)
    near_frames = neighbours(frame_of, 2 * SPAN)
    near_cotangent = neighbours(time_cotangent, SPAN)
    own_rows = slice(2 * SPAN, 2 * SPAN + token_count)
    block_at = lax.axis_index("dev") * blocks - 2 + jnp.arange((blocks + 4) * SPAN) // SPAN
    bias = jnp.where((block_at >= 0) & (block_at < devices * blocks), 0.0, -1e30)[None, :]

    def spatial_forward():
        rows = frames.reshape(frame_count * patches, width).astype(jnp.float32)
        scaled_rows, _ = normalize(rows)
        normed = (scaled_rows * norm_gain).astype(jnp.bfloat16)
        packed = jnp.dot(normed, in_proj, preferred_element_type=jnp.float32).astype(jnp.bfloat16)
        packed = packed.reshape(frame_count, patches, 3, HEADS, HEAD_DIM)
        attention_logits = (
            jnp.einsum(
                "fphd,fqhd->fhpq",
                packed[:, :, 0],
                packed[:, :, 1],
                preferred_element_type=jnp.float32,
            )
            * SCALE
        )
        attention_probs = jax.nn.softmax(attention_logits, axis=-1).astype(jnp.bfloat16)
        attended_output = jnp.einsum(
            "fhpq,fqhd->fphd", attention_probs, packed[:, :, 2], preferred_element_type=jnp.float32
        )
        attended_output = attended_output.astype(jnp.bfloat16).reshape(frame_count * patches, width)
        sums = jnp.sum(
            attended_output.reshape(frame_count, patches, width).astype(jnp.float32), axis=1
        )
        both = jnp.dot(
            jnp.concatenate(halves(sums), axis=0), out_proj, preferred_element_type=jnp.float32
        )
        carried = jnp.mean(rows.reshape(frame_count, patches, width), axis=1)
        pooled = carried + (both[:frame_count] + both[frame_count:]) / patches
        pooled = lined(pooled.astype(jnp.bfloat16).reshape(1, frame_count * width), lines)[0]
        return (pooled, attended_output, sums)

    pooled, spatial_mixed, sums = when_true(spatial, spatial_forward)
    grad_mixed = when_true(
        temporal, lambda: contract_cols(near_cotangent, out_proj).astype(jnp.bfloat16)
    )
    arrived = unlined(spread(pooled, devices), frame_count, width)

    def temporal_forward():
        selector = (near_frames[:, None] == trained[None, :]).astype(jnp.bfloat16)
        inputs = near_tokens.astype(jnp.float32) + jnp.dot(
            selector, arrived, preferred_element_type=jnp.float32
        )
        scaled_rows, inverse = normalize(inputs)
        normed = (scaled_rows * norm_gain).astype(jnp.bfloat16)
        packed = jnp.dot(normed, in_proj, preferred_element_type=jnp.float32).astype(jnp.bfloat16)
        stat = jax.ShapeDtypeStruct(((blocks + 2) * SPAN, 128), jnp.float32)
        time_mixed, log_total, row_delta = local_call(
            attend_kernel,
            (jax.ShapeDtypeStruct((token_count, width), jnp.bfloat16), stat, stat),
            packed, grad_mixed, bias,
        )
        part = contract_rows(time_mixed, time_cotangent).astype(jnp.bfloat16)
        return (
            part, packed, log_total, row_delta,
            selector[own_rows], scaled_rows[own_rows], inverse[own_rows],
        )

    def from_frames():
        part = contract_rows(
            spatial_mixed, patch_cotangent.reshape(frame_count * patches, width)
        ).astype(jnp.bfloat16)
        skipped = jax.tree.map(
            lambda leaf: jnp.zeros(leaf.shape, leaf.dtype), jax.eval_shape(temporal_forward)[1:]
        )
        return (part,) + tuple(skipped)

    part, packed, log_total, row_delta, selector, scaled_rows, inverse = lax.cond(
        spatial, from_frames, temporal_forward
    )
    weight_part = lax.psum_scatter(part, "dev", scatter_dimension=0, tiled=True).astype(jnp.float32)

    def temporal_back():
        grad_packed = local_call(
            grads_kernel,
            jax.ShapeDtypeStruct((token_count, 3 * width), jnp.bfloat16),
            packed, grad_mixed, bias, log_total, row_delta,
        )
        grad_scaled = contract_cols(grad_packed, in_proj) * norm_gain
        grad_inputs = inverse * (
            grad_scaled - scaled_rows * jnp.mean(grad_scaled * scaled_rows, axis=-1, keepdims=True)
        ) + time_cotangent.astype(jnp.float32)
        high, low = halves(grad_inputs)
        grads = contract_rows(selector, high) + contract_rows(selector, low)
        return lined(grads.astype(jnp.bfloat16).reshape(devices, frame_count * width), lines)

    parts = when_true(temporal, temporal_back)
    grad_lines, sum_lines = collect(
        parts, lined(sums.reshape(1, frame_count * width), lines)[0], devices
    )

    def from_pooled():
        frame_grads = unlined(grad_lines, frame_count, width).astype(jnp.float32)
        all_sums = unlined(sum_lines, frame_count, width)
        share = width // devices
        own_sums = lax.dynamic_slice_in_dim(
            all_sums, lax.axis_index("dev") * share, share, axis=1
        )
        return weight_part + contract_exact(own_sums, frame_grads) / patches

    return lax.cond(spatial, from_pooled, lambda: weight_part)[None]


def solution(mesh):
    in_specs = (
        P("dev", None, None),
        P(),
        P("dev"),
        P("dev", None),
        P("grp", None),
        P("grp", None, None),
        P("grp", None, None),
        P("dev", None, None),
        P("dev", None),
    )
    out_specs = P("grp", "dev", None)
    return jax.shard_map(shards, mesh=mesh, in_specs=in_specs, out_specs=out_specs, check_vma=False)
```

```python
import functools

import jax
import jax.numpy as jnp
from jax import lax
from jax.experimental import pallas as pl
from jax.experimental.pallas import tpu as pltpu
from jax.sharding import PartitionSpec as P

HEADS = 16
HEAD_DIM = 88
SPAN = 128


EPS = 1e-06
HIGH_PRECISION = lax.Precision.HIGHEST


def normalize(rows):
    inverse = lax.rsqrt(jnp.mean(rows * rows, axis=-1, keepdims=True) + EPS)
    return (rows * inverse, inverse)


def when_true(flag, compute):

    def skipped():
        return jax.tree.map(jnp.zeros_like, compute())

    return lax.cond(flag, compute, skipped)


def contract_rows(left, right):
    return lax.dot_general(
        left, right, (((0,), (0,)), ((), ())), preferred_element_type=jnp.float32
    )


def contract_exact(left, right):
    return lax.dot_general(left, right, (((0,), (0,)), ((), ())), precision=HIGH_PRECISION)


def halves(value):
    high = lax.reduce_precision(value, 8, 7)
    return high.astype(jnp.bfloat16), (value - high).astype(jnp.bfloat16)


def lined(rows, lines):
    flat = rows.reshape(rows.shape[0], -1)
    return jnp.pad(flat, ((0, 0), (0, lines * 128 - flat.shape[1]))).reshape(-1, lines, 128)


def unlined(lines, count, width):
    flat = lines.reshape(lines.shape[0], -1)[:, : count * width]
    return flat.reshape(lines.shape[0] * count, width)


MESH = pl.DeviceIdType.MESH


def spread_kernel(
    count, own, tokens, grads, frames, out, near_tokens, near_grads, near_frames, send_sem,
    recv_sem, side_send, side_recv,
):
    group = lax.axis_index("grp")
    me = lax.axis_index("dev")
    barrier = pltpu.get_barrier_semaphore()
    extended = ((tokens, near_tokens, 2 * SPAN), (grads, near_grads, SPAN), (frames, near_frames, 2))

    def copy(slot, target, group_to):
        return pltpu.make_async_remote_copy(
            src_ref=own,
            dst_ref=out.at[slot],
            send_sem=send_sem.at[target],
            recv_sem=recv_sem.at[slot],
            device_id=(group_to, target),
            device_id_type=MESH,
        )

    def side_copies(upward, target):
        copies = []
        for at, (source, near, rows) in enumerate(extended):
            length = source.shape[0]
            index = at + 3 * upward
            copies.append(
                pltpu.make_async_remote_copy(
                    src_ref=source.at[pl.ds(length - rows if upward else 0, rows)],
                    dst_ref=near.at[pl.ds(0 if upward else length + rows, rows)],
                    send_sem=side_send.at[index],
                    recv_sem=side_recv.at[index],
                    device_id=(1, target),
                    device_id_type=MESH,
                )
            )
        return copies

    not_first, not_last = me > 0, me < count - 1
    above, below = jnp.minimum(me + 1, count - 1), jnp.maximum(me - 1, 0)

    @pl.when(group == 1)
    def _():
        @pl.loop(0, count)
        def _(j):
            pl.semaphore_signal(barrier, inc=1, device_id=(0, j), device_id_type=MESH)

        @pl.when(not_first)
        def _():
            pl.semaphore_signal(barrier, inc=1, device_id=(1, below), device_id_type=MESH)

        @pl.when(not_last)
        def _():
            pl.semaphore_signal(barrier, inc=1, device_id=(1, above), device_id_type=MESH)

    @pl.when(group == 0)
    def _():
        pl.semaphore_wait(barrier, count)

        @pl.loop(0, count)
        def _(j):
            copy(me, lax.rem(me + j, count), 1).start()

        @pl.loop(0, count)
        def _(j):
            copy(me, lax.rem(me + j, count), 1).wait_send()

    @pl.when(group == 1)
    def _():
        pl.semaphore_wait(barrier, jnp.where(not_first, 1, 0) + jnp.where(not_last, 1, 0))

        @pl.when(not_last)
        def _():
            for side in side_copies(1, above):
                side.start()

        @pl.when(not_first)
        def _():
            for side in side_copies(0, below):
                side.start()

        for source, near, rows in extended:
            near[rows : rows + source.shape[0]] = source[...]

        @pl.when(jnp.logical_not(not_first))
        def _():
            for source, near, rows in extended:
                near[:rows] = jnp.zeros((rows,) + near.shape[1:], near.dtype)

        @pl.when(jnp.logical_not(not_last))
        def _():
            for source, near, rows in extended:
                near[rows + source.shape[0] :] = jnp.zeros((rows,) + near.shape[1:], near.dtype)

        @pl.when(not_first)
        def _():
            for side in side_copies(1, below):
                side.wait_recv()
            for side in side_copies(0, below):
                side.wait_send()

        @pl.when(not_last)
        def _():
            for side in side_copies(0, above):
                side.wait_recv()
            for side in side_copies(1, above):
                side.wait_send()

        @pl.loop(0, count)
        def _(j):
            copy(j, j, 0).wait_recv()


def spread(own, tokens, grads, frames, count):
    vmem = pl.BlockSpec(memory_space=pltpu.VMEM)

    def longer(array, rows):
        return jax.ShapeDtypeStruct((array.shape[0] + 2 * rows,) + array.shape[1:], array.dtype)

    return pl.pallas_call(
        functools.partial(spread_kernel, count),
        out_shape=(
            jax.ShapeDtypeStruct((count,) + own.shape, own.dtype),
            longer(tokens, 2 * SPAN),
            longer(grads, SPAN),
            longer(frames, 2),
        ),
        in_specs=[vmem] * 4,
        out_specs=(vmem,) * 4,
        scratch_shapes=[pltpu.SemaphoreType.DMA((n,)) for n in (count, count, 6, 6)],
        compiler_params=pltpu.CompilerParams(
            collective_id=1, has_side_effects=True, vmem_limit_bytes=32 << 20
        ),
    )(own, tokens, grads, frames)


def collect_kernel(
    count, parts, sums, grads_out, sums_out, landed, part_send, part_recv, sum_send, sum_recv,
    grad_send, grad_recv,
):
    group = lax.axis_index("grp")
    me = lax.axis_index("dev")
    barrier = pltpu.get_barrier_semaphore()

    def part_copy(slot, target, group_to):
        return pltpu.make_async_remote_copy(
            src_ref=parts.at[target],
            dst_ref=landed.at[slot],
            send_sem=part_send.at[target],
            recv_sem=part_recv.at[slot],
            device_id=(group_to, target),
            device_id_type=MESH,
        )

    def sum_copy(slot, target):
        return pltpu.make_async_remote_copy(
            src_ref=sums,
            dst_ref=sums_out.at[slot],
            send_sem=sum_send.at[target],
            recv_sem=sum_recv.at[slot],
            device_id=(0, target),
            device_id_type=MESH,
        )

    def grad_copy(slot, target):
        return pltpu.make_async_remote_copy(
            src_ref=grads_out.at[me],
            dst_ref=grads_out.at[slot],
            send_sem=grad_send.at[target],
            recv_sem=grad_recv.at[slot],
            device_id=(0, target),
            device_id_type=MESH,
        )

    @pl.when(group == 0)
    def _():
        @pl.loop(0, count)
        def _(j):
            pl.semaphore_signal(barrier, inc=1, device_id=(1, j), device_id_type=MESH)

        @pl.loop(1, count)
        def _(j):
            pl.semaphore_signal(
                barrier, inc=1, device_id=(0, lax.rem(me + j, count)), device_id_type=MESH
            )

        pl.semaphore_wait(barrier, count - 1)

        @pl.loop(1, count)
        def _(j):
            sum_copy(me, lax.rem(me + j, count)).start()

        sums_out[me] = sums[...]

        @pl.loop(1, count)
        def _(j):
            other = lax.rem(me + j, count)
            sum_copy(other, other).wait_recv()

        @pl.loop(1, count)
        def _(j):
            sum_copy(me, lax.rem(me + j, count)).wait_send()

    @pl.when(group == 1)
    def _():
        pl.semaphore_wait(barrier, count)

        @pl.loop(0, count)
        def _(j):
            part_copy(me, lax.rem(me + j, count), 0).start()

        @pl.loop(0, count)
        def _(j):
            part_copy(me, lax.rem(me + j, count), 0).wait_send()

    @pl.when(group == 0)
    def _():
        @pl.loop(0, count)
        def _(j):
            part_copy(j, j, 1).wait_recv()

        total = jnp.sum(landed[...].astype(jnp.float32), axis=0)
        grads_out[me] = total.astype(jnp.bfloat16)

        @pl.loop(1, count)
        def _(j):
            grad_copy(me, lax.rem(me + j, count)).start()

        @pl.loop(1, count)
        def _(j):
            other = lax.rem(me + j, count)
            grad_copy(other, other).wait_recv()

        @pl.loop(1, count)
        def _(j):
            grad_copy(me, lax.rem(me + j, count)).wait_send()


def collect(parts, sums, count):
    vmem = pl.BlockSpec(memory_space=pltpu.VMEM)
    return pl.pallas_call(
        functools.partial(collect_kernel, count),
        out_shape=(
            jax.ShapeDtypeStruct(parts.shape, parts.dtype),
            jax.ShapeDtypeStruct((count,) + sums.shape, sums.dtype),
        ),
        in_specs=[vmem, vmem],
        out_specs=(vmem, vmem),
        scratch_shapes=[pltpu.VMEM(parts.shape, parts.dtype)]
        + [pltpu.SemaphoreType.DMA((count,)) for _ in range(6)],
        compiler_params=pltpu.CompilerParams(
            collective_id=2, has_side_effects=True, vmem_limit_bytes=32 << 20
        ),
    )(parts, sums)


def contract_cols(left, right):
    return lax.dot_general(
        left, right, (((1,), (1,)), ((), ())), preferred_element_type=jnp.float32
    )


def dot_cols(left, right):
    return lax.dot_general(
        left, right, (((1,), (1,)), ((), ())), preferred_element_type=jnp.float32
    )


def dot_rows(left, right):
    return lax.dot_general(
        left, right, (((0,), (0,)), ((), ())), preferred_element_type=jnp.float32
    )


def dot_plain(left, right):
    return jnp.dot(left, right, preferred_element_type=jnp.float32)


SCALE = HEAD_DIM ** (-0.5)
WINDOW = 256


def block(index, count=1):
    return slice(index * SPAN, (index + count) * SPAN)


def head_window(head, width):
    first = head * HEAD_DIM
    start = pl.multiple_of(jnp.minimum(first // 128, (width - WINDOW) // 128) * 128, 128)
    lane = lax.broadcasted_iota(jnp.int32, (1, WINDOW), 1) + start
    return start, (lane >= first) & (lane < first + HEAD_DIM)


def blend(ref, rows, columns, mask, value):
    old = ref[rows, columns].astype(jnp.float32)
    ref[rows, columns] = jnp.where(mask, value, old).astype(ref.dtype)


def attend_kernel(packed, grad, bias, mixed, log_total, row_delta):
    width = grad.shape[1]
    blocks = grad.shape[0] // SPAN
    lanes = lax.broadcasted_iota(jnp.int32, (1, 128), 1)

    def one_head(head, carry):
        start, mask = head_window(head, width)
        keep = mask.astype(jnp.float32).astype(jnp.bfloat16)
        here = pl.ds(start, WINDOW)
        key_at = pl.ds(pl.multiple_of(start + width, 128), WINDOW)
        value_at = pl.ds(pl.multiple_of(start + 2 * width, 128), WINDOW)
        for i in range(blocks):
            query = packed[block(i + 1), here] * keep
            logits = dot_cols(query, packed[block(i, 3), key_at]) + bias[:, block(i, 3)]
            top = jnp.max(logits, axis=-1, keepdims=True)
            raised = jnp.exp((logits - top) * SCALE)
            total = jnp.sum(raised, axis=-1, keepdims=True)
            chances = (raised * (1.0 / total)).astype(jnp.bfloat16)
            value = dot_plain(chances, packed[block(i, 3), value_at])
            rounded = value.astype(jnp.bfloat16).astype(jnp.float32)
            product = grad[block(i), here].astype(jnp.float32) * rounded
            delta = jnp.sum(jnp.where(mask, product, 0.0), axis=-1, keepdims=True)
            own = lanes == head
            every = slice(0, 128)
            blend(log_total, block(i), every, own, top * SCALE + jnp.log(total))
            blend(row_delta, block(i), every, own, delta)
            if 1 <= i < blocks - 1:
                blend(mixed, block(i - 1), here, mask, value)
        return carry

    lax.fori_loop(0, HEADS, one_head, 0, unroll=2)


def grads_kernel(packed, grad, bias, log_total, row_delta, out):
    width = grad.shape[1]
    blocks = grad.shape[0] // SPAN
    lanes = lax.broadcasted_iota(jnp.int32, (1, 128), 1)

    def one_head(head, carry):
        start, mask = head_window(head, width)
        keep = mask.astype(jnp.float32).astype(jnp.bfloat16)
        here = pl.ds(start, WINDOW)
        key_at = pl.ds(pl.multiple_of(start + width, 128), WINDOW)
        value_at = pl.ds(pl.multiple_of(start + 2 * width, 128), WINDOW)
        own = lanes == head
        query = packed[block(1, blocks), here] * keep
        cotangent = grad[:, here] * keep
        chance_of, grad_of = {}, {}
        for i in range(blocks):
            if i == 0:
                first, span = 1, 1
            elif i == blocks - 1:
                first, span = blocks - 2, 1
            else:
                first, span = i - 1, 3
            at = block(first + 1, span)
            inside = bias[:, at] if span == 3 else bias[:, block(i + 1)]
            total = jnp.sum(jnp.where(own, log_total[block(i), :], 0.0), axis=-1, keepdims=True)
            delta = jnp.sum(jnp.where(own, row_delta[block(i), :], 0.0), axis=-1, keepdims=True)
            keys = packed[at, key_at]
            logits = dot_cols(query[block(i)], keys) * SCALE + inside
            chances = jnp.exp(logits - total)
            slope = dot_cols(cotangent[block(i)], packed[at, value_at])
            logit_grad = (chances * (slope - delta)).astype(jnp.bfloat16)
            chances = chances.astype(jnp.bfloat16)
            for step in range(span):
                chance_of[i, first + step] = chances[:, block(step)]
                grad_of[i, first + step] = logit_grad[:, block(step)]
            if span == 3:
                blend(out, block(i - 1), here, mask, dot_plain(logit_grad, keys) * SCALE)
        for j in range(1, blocks - 1):
            rows = block(j - 1, 3)
            near = range(j - 1, j + 2)
            scores = jnp.concatenate([grad_of[i, j] for i in near], axis=0)
            blend(out, block(j - 1), key_at, mask, dot_rows(scores, query[rows]) * SCALE)
            weights = jnp.concatenate([chance_of[i, j] for i in near], axis=0)
            blend(out, block(j - 1), value_at, mask, dot_rows(weights, cotangent[rows]))
        return carry

    lax.fori_loop(0, HEADS, one_head, 0, unroll=2)


def local_call(kernel, out_shape, *operands):
    return pl.pallas_call(
        kernel,
        out_shape=out_shape,
        in_specs=[pl.BlockSpec(memory_space=pltpu.VMEM)] * len(operands),
        out_specs=jax.tree.map(lambda _: pl.BlockSpec(memory_space=pltpu.VMEM), out_shape),
        compiler_params=pltpu.CompilerParams(vmem_limit_bytes=48 << 20),
    )(*operands)


def shards(
    frames,
    trained,
    frame_of,
    token_cache,
    norm_gains,
    proj_weights,
    out_weights,
    patch_cotangent,
    time_cotangent,
):
    spatial = lax.axis_index("grp") == 0
    temporal = jnp.logical_not(spatial)
    norm_gain = norm_gains[0]
    in_proj = proj_weights[0]
    out_proj = out_weights[0]
    width = in_proj.shape[0]
    frame_count, patches, _ = frames.shape
    token_count = token_cache.shape[0]
    devices = lax.axis_size("dev")
    lines = -(-frame_count * width // 2048) * 16
    blocks = token_count // SPAN
    own_rows = slice(2 * SPAN, 2 * SPAN + token_count)
    block_at = lax.axis_index("dev") * blocks - 2 + jnp.arange((blocks + 4) * SPAN) // SPAN
    bias = jnp.where((block_at >= 0) & (block_at < devices * blocks), 0.0, -1e30)[None, :]

    def spatial_forward():
        rows = frames.reshape(frame_count * patches, width).astype(jnp.float32)
        scaled_rows, _ = normalize(rows)
        normed = (scaled_rows * norm_gain).astype(jnp.bfloat16)
        packed = jnp.dot(normed, in_proj, preferred_element_type=jnp.float32).astype(jnp.bfloat16)
        packed = packed.reshape(frame_count, patches, 3, HEADS, HEAD_DIM)
        attention_logits = (
            jnp.einsum(
                "fphd,fqhd->fhpq",
                packed[:, :, 0],
                packed[:, :, 1],
                preferred_element_type=jnp.float32,
            )
            * SCALE
        )
        attention_probs = jax.nn.softmax(attention_logits, axis=-1).astype(jnp.bfloat16)
        attended_output = jnp.einsum(
            "fhpq,fqhd->fphd", attention_probs, packed[:, :, 2], preferred_element_type=jnp.float32
        )
        attended_output = attended_output.astype(jnp.bfloat16).reshape(frame_count * patches, width)
        sums = jnp.sum(
            attended_output.reshape(frame_count, patches, width).astype(jnp.float32), axis=1
        )
        both = jnp.dot(
            jnp.concatenate(halves(sums), axis=0), out_proj, preferred_element_type=jnp.float32
        )
        carried = jnp.mean(rows.reshape(frame_count, patches, width), axis=1)
        pooled = carried + (both[:frame_count] + both[frame_count:]) / patches
        pooled = lined(pooled.astype(jnp.bfloat16).reshape(1, frame_count * width), lines)[0]
        grad_mixed = jnp.zeros((token_count, width), jnp.bfloat16)
        return (pooled, attended_output, sums, grad_mixed)

    def ahead():
        return (
            jnp.zeros((lines, 128), jnp.bfloat16),
            jnp.zeros((frame_count * patches, width), jnp.bfloat16),
            jnp.zeros((frame_count, width), jnp.float32),
            contract_cols(time_cotangent, out_proj).astype(jnp.bfloat16),
        )

    pooled, spatial_mixed, sums, own_grad = lax.cond(spatial, spatial_forward, ahead)
    frame_lines = jnp.broadcast_to(frame_of.reshape(blocks, 1, SPAN), (blocks, 8, SPAN))
    arrived, near_tokens, grad_mixed, near_lines = spread(
        pooled, token_cache, own_grad, frame_lines, devices
    )
    arrived = unlined(arrived, frame_count, width)
    near_frames = near_lines[:, 0].reshape(-1)

    def temporal_forward():
        selector = (near_frames[:, None] == trained[None, :]).astype(jnp.bfloat16)
        inputs = near_tokens.astype(jnp.float32) + jnp.dot(
            selector, arrived, preferred_element_type=jnp.float32
        )
        scaled_rows, inverse = normalize(inputs)
        normed = (scaled_rows * norm_gain).astype(jnp.bfloat16)
        packed = jnp.dot(normed, in_proj, preferred_element_type=jnp.float32).astype(jnp.bfloat16)
        stat = jax.ShapeDtypeStruct(((blocks + 2) * SPAN, 128), jnp.float32)
        time_mixed, log_total, row_delta = local_call(
            attend_kernel,
            (jax.ShapeDtypeStruct((token_count, width), jnp.bfloat16), stat, stat),
            packed, grad_mixed, bias,
        )
        part = contract_rows(time_mixed, time_cotangent).astype(jnp.bfloat16)
        return (
            part, packed, log_total, row_delta,
            selector[own_rows], scaled_rows[own_rows], inverse[own_rows],
        )

    def from_frames():
        part = contract_rows(
            spatial_mixed, patch_cotangent.reshape(frame_count * patches, width)
        ).astype(jnp.bfloat16)
        skipped = jax.tree.map(
            lambda leaf: jnp.zeros(leaf.shape, leaf.dtype), jax.eval_shape(temporal_forward)[1:]
        )
        return (part,) + tuple(skipped)

    part, packed, log_total, row_delta, selector, scaled_rows, inverse = lax.cond(
        spatial, from_frames, temporal_forward
    )
    core = lax.rem(lax.axis_index("dev"), 2)
    part = part.reshape(devices // 2, 2, width // devices, width)
    kept = lax.dynamic_index_in_dim(part, core, axis=1, keepdims=False)
    given = lax.dynamic_index_in_dim(part, 1 - core, axis=1, keepdims=False)
    taken = lax.ppermute(given, "dev", [(i, i ^ 1) for i in range(devices)])
    pair = (kept.astype(jnp.float32) + taken.astype(jnp.float32)).astype(jnp.bfloat16)
    weight_part = lax.psum_scatter(
        pair.reshape(width // 2, width),
        "dev",
        scatter_dimension=0,
        axis_index_groups=[list(range(start, devices, 2)) for start in range(2)],
        tiled=True,
    ).astype(jnp.float32)

    def temporal_back():
        grad_packed = local_call(
            grads_kernel,
            jax.ShapeDtypeStruct((token_count, 3 * width), jnp.bfloat16),
            packed, grad_mixed, bias, log_total, row_delta,
        )
        grad_scaled = contract_cols(grad_packed, in_proj) * norm_gain
        grad_inputs = inverse * (
            grad_scaled - scaled_rows * jnp.mean(grad_scaled * scaled_rows, axis=-1, keepdims=True)
        ) + time_cotangent.astype(jnp.float32)
        high, low = halves(grad_inputs)
        grads = contract_rows(selector, high) + contract_rows(selector, low)
        return lined(grads.astype(jnp.bfloat16).reshape(devices, frame_count * width), lines)

    parts = when_true(temporal, temporal_back)
    grad_lines, sum_lines = collect(
        parts, lined(sums.reshape(1, frame_count * width), lines)[0], devices
    )

    def from_pooled():
        frame_grads = unlined(grad_lines, frame_count, width).astype(jnp.float32)
        all_sums = unlined(sum_lines, frame_count, width)
        share = width // devices
        own_sums = lax.dynamic_slice_in_dim(
            all_sums, lax.axis_index("dev") * share, share, axis=1
        )
        return weight_part + contract_exact(own_sums, frame_grads) / patches

    return lax.cond(spatial, from_pooled, lambda: weight_part)[None]


def solution(mesh):
    in_specs = (
        P("dev", None, None),
        P(),
        P("dev"),
        P("dev", None),
        P("grp", None),
        P("grp", None, None),
        P("grp", None, None),
        P("dev", None, None),
        P("dev", None),
    )
    out_specs = P("grp", "dev", None)
    return jax.shard_map(shards, mesh=mesh, in_specs=in_specs, out_specs=out_specs, check_vma=False)
```

```python
import functools

import jax
import jax.numpy as jnp
from jax import lax
from jax.experimental import pallas as pl
from jax.experimental.pallas import tpu as pltpu
from jax.sharding import PartitionSpec as P

HEADS = 16
HEAD_DIM = 88
SPAN = 128


EPS = 1e-06
HIGH_PRECISION = lax.Precision.HIGHEST


def normalize(rows):
    inverse = lax.rsqrt(jnp.mean(rows * rows, axis=-1, keepdims=True) + EPS)
    return (rows * inverse, inverse)


def when_true(flag, compute):

    def skipped():
        return jax.tree.map(jnp.zeros_like, compute())

    return lax.cond(flag, compute, skipped)


def contract_rows(left, right):
    return lax.dot_general(
        left, right, (((0,), (0,)), ((), ())), preferred_element_type=jnp.float32
    )


def contract_exact(left, right):
    return lax.dot_general(left, right, (((0,), (0,)), ((), ())), precision=HIGH_PRECISION)


def halves(value):
    high = lax.reduce_precision(value, 8, 7)
    return high.astype(jnp.bfloat16), (value - high).astype(jnp.bfloat16)


def lined(rows, lines):
    flat = rows.reshape(rows.shape[0], -1)
    return jnp.pad(flat, ((0, 0), (0, lines * 128 - flat.shape[1]))).reshape(-1, lines, 128)


def unlined(lines, count, width):
    flat = lines.reshape(lines.shape[0], -1)[:, : count * width]
    return flat.reshape(lines.shape[0] * count, width)


MESH = pl.DeviceIdType.MESH


def spread_kernel(
    count, own, tokens, grads, frames, out, near_tokens, near_grads, near_frames, send_sem,
    recv_sem, side_send, side_recv,
):
    group = lax.axis_index("grp")
    me = lax.axis_index("dev")
    barrier = pltpu.get_barrier_semaphore()
    extended = ((tokens, near_tokens, 2 * SPAN), (grads, near_grads, SPAN), (frames, near_frames, 2))

    def copy(slot, target, group_to):
        return pltpu.make_async_remote_copy(
            src_ref=own,
            dst_ref=out.at[slot],
            send_sem=send_sem.at[target],
            recv_sem=recv_sem.at[slot],
            device_id=(group_to, target),
            device_id_type=MESH,
        )

    def side_copies(upward, target):
        copies = []
        for at, (source, near, rows) in enumerate(extended):
            length = source.shape[0]
            index = at + 3 * upward
            copies.append(
                pltpu.make_async_remote_copy(
                    src_ref=source.at[pl.ds(length - rows if upward else 0, rows)],
                    dst_ref=near.at[pl.ds(0 if upward else length + rows, rows)],
                    send_sem=side_send.at[index],
                    recv_sem=side_recv.at[index],
                    device_id=(1, target),
                    device_id_type=MESH,
                )
            )
        return copies

    not_first, not_last = me > 0, me < count - 1
    above, below = jnp.minimum(me + 1, count - 1), jnp.maximum(me - 1, 0)

    @pl.when(group == 1)
    def _():
        @pl.loop(0, count)
        def _(j):
            pl.semaphore_signal(barrier, inc=1, device_id=(0, j), device_id_type=MESH)

        @pl.when(not_first)
        def _():
            pl.semaphore_signal(barrier, inc=1, device_id=(1, below), device_id_type=MESH)

        @pl.when(not_last)
        def _():
            pl.semaphore_signal(barrier, inc=1, device_id=(1, above), device_id_type=MESH)

    @pl.when(group == 0)
    def _():
        pl.semaphore_wait(barrier, count)

        @pl.loop(0, count)
        def _(j):
            copy(me, lax.rem(me + j, count), 1).start()

        @pl.loop(0, count)
        def _(j):
            copy(me, lax.rem(me + j, count), 1).wait_send()

    @pl.when(group == 1)
    def _():
        pl.semaphore_wait(barrier, jnp.where(not_first, 1, 0) + jnp.where(not_last, 1, 0))

        @pl.when(not_last)
        def _():
            for side in side_copies(1, above):
                side.start()

        @pl.when(not_first)
        def _():
            for side in side_copies(0, below):
                side.start()

        for source, near, rows in extended:
            near[rows : rows + source.shape[0]] = source[...]

        @pl.when(jnp.logical_not(not_first))
        def _():
            for source, near, rows in extended:
                near[:rows] = jnp.zeros((rows,) + near.shape[1:], near.dtype)

        @pl.when(jnp.logical_not(not_last))
        def _():
            for source, near, rows in extended:
                near[rows + source.shape[0] :] = jnp.zeros((rows,) + near.shape[1:], near.dtype)

        @pl.when(not_first)
        def _():
            for side in side_copies(1, below):
                side.wait_recv()
            for side in side_copies(0, below):
                side.wait_send()

        @pl.when(not_last)
        def _():
            for side in side_copies(0, above):
                side.wait_recv()
            for side in side_copies(1, above):
                side.wait_send()

        @pl.loop(0, count)
        def _(j):
            copy(j, j, 0).wait_recv()


def spread(own, tokens, grads, frames, count):
    vmem = pl.BlockSpec(memory_space=pltpu.VMEM)

    def longer(array, rows):
        return jax.ShapeDtypeStruct((array.shape[0] + 2 * rows,) + array.shape[1:], array.dtype)

    return pl.pallas_call(
        functools.partial(spread_kernel, count),
        out_shape=(
            jax.ShapeDtypeStruct((count,) + own.shape, own.dtype),
            longer(tokens, 2 * SPAN),
            longer(grads, SPAN),
            longer(frames, 2),
        ),
        in_specs=[vmem] * 4,
        out_specs=(vmem,) * 4,
        scratch_shapes=[pltpu.SemaphoreType.DMA((n,)) for n in (count, count, 6, 6)],
        compiler_params=pltpu.CompilerParams(
            collective_id=1, has_side_effects=True, vmem_limit_bytes=32 << 20
        ),
    )(own, tokens, grads, frames)


def collect_kernel(
    count, parts, sums, grads_out, sums_out, landed, part_send, part_recv, sum_send, sum_recv,
    grad_send, grad_recv,
):
    group = lax.axis_index("grp")
    me = lax.axis_index("dev")
    barrier = pltpu.get_barrier_semaphore()

    def part_copy(slot, target, group_to):
        return pltpu.make_async_remote_copy(
            src_ref=parts.at[target],
            dst_ref=landed.at[slot],
            send_sem=part_send.at[target],
            recv_sem=part_recv.at[slot],
            device_id=(group_to, target),
            device_id_type=MESH,
        )

    def sum_copy(slot, target):
        return pltpu.make_async_remote_copy(
            src_ref=sums,
            dst_ref=sums_out.at[slot],
            send_sem=sum_send.at[target],
            recv_sem=sum_recv.at[slot],
            device_id=(0, target),
            device_id_type=MESH,
        )

    def grad_copy(slot, target):
        return pltpu.make_async_remote_copy(
            src_ref=grads_out.at[me],
            dst_ref=grads_out.at[slot],
            send_sem=grad_send.at[target],
            recv_sem=grad_recv.at[slot],
            device_id=(0, target),
            device_id_type=MESH,
        )

    @pl.when(group == 0)
    def _():
        @pl.loop(0, count)
        def _(j):
            pl.semaphore_signal(barrier, inc=1, device_id=(1, j), device_id_type=MESH)

        @pl.loop(1, count)
        def _(j):
            pl.semaphore_signal(
                barrier, inc=1, device_id=(0, lax.rem(me + j, count)), device_id_type=MESH
            )

        pl.semaphore_wait(barrier, count - 1)

        @pl.loop(1, count)
        def _(j):
            sum_copy(me, lax.rem(me + j, count)).start()

        sums_out[me] = sums[...]

        @pl.loop(1, count)
        def _(j):
            other = lax.rem(me + j, count)
            sum_copy(other, other).wait_recv()

        @pl.loop(1, count)
        def _(j):
            sum_copy(me, lax.rem(me + j, count)).wait_send()

    @pl.when(group == 1)
    def _():
        pl.semaphore_wait(barrier, count)

        @pl.loop(0, count)
        def _(j):
            part_copy(me, lax.rem(me + j, count), 0).start()

        @pl.loop(0, count)
        def _(j):
            part_copy(me, lax.rem(me + j, count), 0).wait_send()

    @pl.when(group == 0)
    def _():
        @pl.loop(0, count)
        def _(j):
            part_copy(j, j, 1).wait_recv()

        total = jnp.sum(landed[...].astype(jnp.float32), axis=0)
        grads_out[me] = total.astype(jnp.bfloat16)

        @pl.loop(1, count)
        def _(j):
            grad_copy(me, lax.rem(me + j, count)).start()

        @pl.loop(1, count)
        def _(j):
            other = lax.rem(me + j, count)
            grad_copy(other, other).wait_recv()

        @pl.loop(1, count)
        def _(j):
            grad_copy(me, lax.rem(me + j, count)).wait_send()


def collect(parts, sums, count):
    vmem = pl.BlockSpec(memory_space=pltpu.VMEM)
    return pl.pallas_call(
        functools.partial(collect_kernel, count),
        out_shape=(
            jax.ShapeDtypeStruct(parts.shape, parts.dtype),
            jax.ShapeDtypeStruct((count,) + sums.shape, sums.dtype),
        ),
        in_specs=[vmem, vmem],
        out_specs=(vmem, vmem),
        scratch_shapes=[pltpu.VMEM(parts.shape, parts.dtype)]
        + [pltpu.SemaphoreType.DMA((count,)) for _ in range(6)],
        compiler_params=pltpu.CompilerParams(
            collective_id=2, has_side_effects=True, vmem_limit_bytes=32 << 20
        ),
    )(parts, sums)


def contract_cols(left, right):
    return lax.dot_general(
        left, right, (((1,), (1,)), ((), ())), preferred_element_type=jnp.float32
    )


def dot_cols(left, right):
    return lax.dot_general(
        left, right, (((1,), (1,)), ((), ())), preferred_element_type=jnp.float32
    )


def dot_rows(left, right):
    return lax.dot_general(
        left, right, (((0,), (0,)), ((), ())), preferred_element_type=jnp.float32
    )


def dot_plain(left, right):
    return jnp.dot(left, right, preferred_element_type=jnp.float32)


SCALE = HEAD_DIM ** (-0.5)
WINDOW = 256


def block(index, count=1):
    return slice(index * SPAN, (index + count) * SPAN)


def head_window(head, width):
    first = head * HEAD_DIM
    start = pl.multiple_of(jnp.minimum(first // 128, (width - WINDOW) // 128) * 128, 128)
    lane = lax.broadcasted_iota(jnp.int32, (1, WINDOW), 1) + start
    return start, (lane >= first) & (lane < first + HEAD_DIM)


def blend(ref, rows, columns, mask, value):
    old = ref[rows, columns].astype(jnp.float32)
    ref[rows, columns] = jnp.where(mask, value, old).astype(ref.dtype)


def attend_kernel(chosen, packed, grad, bias, log_total, row_delta, mixed=None):
    width = grad.shape[1]
    lanes = lax.broadcasted_iota(jnp.int32, (1, 128), 1)

    def one_head(head, carry):
        start, mask = head_window(head, width)
        keep = mask.astype(jnp.float32).astype(jnp.bfloat16)
        here = pl.ds(start, WINDOW)
        key_at = pl.ds(pl.multiple_of(start + width, 128), WINDOW)
        value_at = pl.ds(pl.multiple_of(start + 2 * width, 128), WINDOW)
        for place, i in enumerate(chosen):
            query = packed[block(i + 1), here] * keep
            logits = dot_cols(query, packed[block(i, 3), key_at]) + bias[:, block(i, 3)]
            top = jnp.max(logits, axis=-1, keepdims=True)
            raised = jnp.exp((logits - top) * SCALE)
            total = jnp.sum(raised, axis=-1, keepdims=True)
            chances = (raised * (1.0 / total)).astype(jnp.bfloat16)
            value = dot_plain(chances, packed[block(i, 3), value_at])
            rounded = value.astype(jnp.bfloat16).astype(jnp.float32)
            product = grad[block(i), here].astype(jnp.float32) * rounded
            delta = jnp.sum(jnp.where(mask, product, 0.0), axis=-1, keepdims=True)
            own = lanes == head
            every = slice(0, 128)
            blend(log_total, block(place), every, own, top * SCALE + jnp.log(total))
            blend(row_delta, block(place), every, own, delta)
            if mixed is not None:
                blend(mixed, block(place), here, mask, value)
        return carry

    lax.fori_loop(0, HEADS, one_head, 0, unroll=2)


def grads_kernel(packed, grad, bias, log_total, row_delta, out):
    width = grad.shape[1]
    blocks = grad.shape[0] // SPAN
    lanes = lax.broadcasted_iota(jnp.int32, (1, 128), 1)

    def one_head(head, carry):
        start, mask = head_window(head, width)
        keep = mask.astype(jnp.float32).astype(jnp.bfloat16)
        here = pl.ds(start, WINDOW)
        key_at = pl.ds(pl.multiple_of(start + width, 128), WINDOW)
        value_at = pl.ds(pl.multiple_of(start + 2 * width, 128), WINDOW)
        own = lanes == head
        query = packed[block(1, blocks), here] * keep
        cotangent = grad[:, here] * keep
        chance_of, grad_of = {}, {}
        for i in range(blocks):
            if i == 0:
                first, span = 1, 1
            elif i == blocks - 1:
                first, span = blocks - 2, 1
            else:
                first, span = i - 1, 3
            at = block(first + 1, span)
            inside = bias[:, at] if span == 3 else bias[:, block(i + 1)]
            total = jnp.sum(jnp.where(own, log_total[block(i), :], 0.0), axis=-1, keepdims=True)
            delta = jnp.sum(jnp.where(own, row_delta[block(i), :], 0.0), axis=-1, keepdims=True)
            keys = packed[at, key_at]
            logits = dot_cols(query[block(i)], keys) * SCALE + inside
            chances = jnp.exp(logits - total)
            slope = dot_cols(cotangent[block(i)], packed[at, value_at])
            logit_grad = (chances * (slope - delta)).astype(jnp.bfloat16)
            chances = chances.astype(jnp.bfloat16)
            for step in range(span):
                chance_of[i, first + step] = chances[:, block(step)]
                grad_of[i, first + step] = logit_grad[:, block(step)]
            if span == 3:
                blend(out, block(i - 1), here, mask, dot_plain(logit_grad, keys) * SCALE)
        for j in range(1, blocks - 1):
            rows = block(j - 1, 3)
            near = range(j - 1, j + 2)
            scores = jnp.concatenate([grad_of[i, j] for i in near], axis=0)
            blend(out, block(j - 1), key_at, mask, dot_rows(scores, query[rows]) * SCALE)
            weights = jnp.concatenate([chance_of[i, j] for i in near], axis=0)
            blend(out, block(j - 1), value_at, mask, dot_rows(weights, cotangent[rows]))
        return carry

    lax.fori_loop(0, HEADS, one_head, 0, unroll=2)


def local_call(kernel, out_shape, *operands):
    return pl.pallas_call(
        kernel,
        out_shape=out_shape,
        in_specs=[pl.BlockSpec(memory_space=pltpu.VMEM)] * len(operands),
        out_specs=jax.tree.map(lambda _: pl.BlockSpec(memory_space=pltpu.VMEM), out_shape),
        compiler_params=pltpu.CompilerParams(vmem_limit_bytes=48 << 20),
    )(*operands)


def shards(
    frames,
    trained,
    frame_of,
    token_cache,
    norm_gains,
    proj_weights,
    out_weights,
    patch_cotangent,
    time_cotangent,
):
    spatial = lax.axis_index("grp") == 0
    temporal = jnp.logical_not(spatial)
    norm_gain = norm_gains[0]
    in_proj = proj_weights[0]
    out_proj = out_weights[0]
    width = in_proj.shape[0]
    frame_count, patches, _ = frames.shape
    token_count = token_cache.shape[0]
    devices = lax.axis_size("dev")
    lines = -(-frame_count * width // 2048) * 16
    blocks = token_count // SPAN
    own_rows = slice(2 * SPAN, 2 * SPAN + token_count)
    block_at = lax.axis_index("dev") * blocks - 2 + jnp.arange((blocks + 4) * SPAN) // SPAN
    bias = jnp.where((block_at >= 0) & (block_at < devices * blocks), 0.0, -1e30)[None, :]

    def spatial_forward():
        rows = frames.reshape(frame_count * patches, width).astype(jnp.float32)
        scaled_rows, _ = normalize(rows)
        normed = (scaled_rows * norm_gain).astype(jnp.bfloat16)
        packed = jnp.dot(normed, in_proj, preferred_element_type=jnp.float32).astype(jnp.bfloat16)
        packed = packed.reshape(frame_count, patches, 3, HEADS, HEAD_DIM)
        attention_logits = (
            jnp.einsum(
                "fphd,fqhd->fhpq",
                packed[:, :, 0],
                packed[:, :, 1],
                preferred_element_type=jnp.float32,
            )
            * SCALE
        )
        attention_probs = jax.nn.softmax(attention_logits, axis=-1).astype(jnp.bfloat16)
        attended_output = jnp.einsum(
            "fhpq,fqhd->fphd", attention_probs, packed[:, :, 2], preferred_element_type=jnp.float32
        )
        attended_output = attended_output.astype(jnp.bfloat16).reshape(frame_count * patches, width)
        sums = jnp.sum(
            attended_output.reshape(frame_count, patches, width).astype(jnp.float32), axis=1
        )
        both = jnp.dot(
            jnp.concatenate(halves(sums), axis=0), out_proj, preferred_element_type=jnp.float32
        )
        carried = jnp.mean(rows.reshape(frame_count, patches, width), axis=1)
        pooled = carried + (both[:frame_count] + both[frame_count:]) / patches
        pooled = lined(pooled.astype(jnp.bfloat16).reshape(1, frame_count * width), lines)[0]
        grad_mixed = jnp.zeros((token_count, width), jnp.bfloat16)
        return (pooled, attended_output, sums, grad_mixed)

    def ahead():
        return (
            jnp.zeros((lines, 128), jnp.bfloat16),
            jnp.zeros((frame_count * patches, width), jnp.bfloat16),
            jnp.zeros((frame_count, width), jnp.float32),
            contract_cols(time_cotangent, out_proj).astype(jnp.bfloat16),
        )

    pooled, spatial_mixed, sums, own_grad = lax.cond(spatial, spatial_forward, ahead)
    frame_lines = jnp.broadcast_to(frame_of.reshape(blocks, 1, SPAN), (blocks, 8, SPAN))
    arrived, near_tokens, grad_mixed, near_lines = spread(
        pooled, token_cache, own_grad, frame_lines, devices
    )
    arrived = unlined(arrived, frame_count, width)
    near_frames = near_lines[:, 0].reshape(-1)

    def temporal_forward():
        selector = (near_frames[:, None] == trained[None, :]).astype(jnp.bfloat16)
        inputs = near_tokens.astype(jnp.float32) + jnp.dot(
            selector, arrived, preferred_element_type=jnp.float32
        )
        scaled_rows, inverse = normalize(inputs)
        normed = (scaled_rows * norm_gain).astype(jnp.bfloat16)
        packed = jnp.dot(normed, in_proj, preferred_element_type=jnp.float32).astype(jnp.bfloat16)
        stat = jax.ShapeDtypeStruct((blocks * SPAN, 128), jnp.float32)
        log_total, row_delta, time_mixed = local_call(
            functools.partial(attend_kernel, range(1, blocks + 1)),
            (stat, stat, jax.ShapeDtypeStruct((token_count, width), jnp.bfloat16)),
            packed, grad_mixed, bias,
        )
        part = contract_rows(time_mixed, time_cotangent).astype(jnp.bfloat16)
        return (
            part, packed, log_total, row_delta,
            selector[own_rows], scaled_rows[own_rows], inverse[own_rows],
        )

    def from_frames():
        part = contract_rows(
            spatial_mixed, patch_cotangent.reshape(frame_count * patches, width)
        ).astype(jnp.bfloat16)
        skipped = jax.tree.map(
            lambda leaf: jnp.zeros(leaf.shape, leaf.dtype), jax.eval_shape(temporal_forward)[1:]
        )
        return (part,) + tuple(skipped)

    part, packed, log_total, row_delta, selector, scaled_rows, inverse = lax.cond(
        spatial, from_frames, temporal_forward
    )
    weight_part = lax.psum_scatter(part, "dev", scatter_dimension=0, tiled=True).astype(jnp.float32)

    def temporal_back():
        stat = jax.ShapeDtypeStruct((2 * SPAN, 128), jnp.float32)
        sides = local_call(
            functools.partial(attend_kernel, (0, blocks + 1)),
            (stat, stat),
            packed, grad_mixed, bias,
        )
        stats = [
            jnp.concatenate([side[:SPAN], own, side[SPAN:]], axis=0)
            for side, own in zip(sides, (log_total, row_delta))
        ]
        grad_packed = local_call(
            grads_kernel,
            jax.ShapeDtypeStruct((token_count, 3 * width), jnp.bfloat16),
            packed, grad_mixed, bias, *stats,
        )
        grad_scaled = contract_cols(grad_packed, in_proj) * norm_gain
        grad_inputs = inverse * (
            grad_scaled - scaled_rows * jnp.mean(grad_scaled * scaled_rows, axis=-1, keepdims=True)
        ) + time_cotangent.astype(jnp.float32)
        high, low = halves(grad_inputs)
        grads = contract_rows(selector, high) + contract_rows(selector, low)
        return lined(grads.astype(jnp.bfloat16).reshape(devices, frame_count * width), lines)

    parts = when_true(temporal, temporal_back)
    grad_lines, sum_lines = collect(
        parts, lined(sums.reshape(1, frame_count * width), lines)[0], devices
    )

    def from_pooled():
        frame_grads = unlined(grad_lines, frame_count, width).astype(jnp.float32)
        all_sums = unlined(sum_lines, frame_count, width)
        share = width // devices
        own_sums = lax.dynamic_slice_in_dim(
            all_sums, lax.axis_index("dev") * share, share, axis=1
        )
        return weight_part + contract_exact(own_sums, frame_grads) / patches

    return lax.cond(spatial, from_pooled, lambda: weight_part)[None]


def solution(mesh):
    in_specs = (
        P("dev", None, None),
        P(),
        P("dev"),
        P("dev", None),
        P("grp", None),
        P("grp", None, None),
        P("grp", None, None),
        P("dev", None, None),
        P("dev", None),
    )
    out_specs = P("grp", "dev", None)
    return jax.shard_map(shards, mesh=mesh, in_specs=in_specs, out_specs=out_specs, check_vma=False)
```
